256 devices in a mesh: row: 16 (over x, z_lo, core), col: 16 (over z_hi, y).
Axes of the slice: x: 4, y: 4, z: 8 (z_hi: 4, z_lo: 2; z = z_hi * 2 + z_lo), core: 2. Of those that a mesh axis runs over, the one named last changes fastest.
Arguments:
- jacobian: bfloat16 [16, 16, 56, 320, 320], P('row', 'col'), may hold values from -3 to 3
- prolong: bfloat16 [2048, 64, 320], P(('row', 'col')), may hold values from -0.3125 to 0.3125
- tile_rows: int32 [16, 16, 56], P('row', 'col'), may hold values from 0 to 127, as said below
- tile_cols: int32 [16, 16, 56], P('row', 'col'), may hold values from 0 to 127
- coarse_slot: int32 [16, 16, 56], P('row', 'col'), may hold values from 0 to 1
Outputs:
- coarse: float32 [16, 16, 64, 128], P('row', 'col')
The draws below stay inside these ranges and needn't reach their ends.
Inputs may be any that keep to these rules, and one draw needn't show every extreme that they name: On every device at most 5 tiles have tile_rows // 8 equal to one value, and exactly 5 for some value.
All inputs are finite; a program needn't handle non-finite values.
Results may differ from the reference program's by a relative error of at most 0.0029.
Values may be sent and summed in bfloat16 or wider, within the bound.
A program may use at most 64 MiB of HBM per device.

```python
import jax
import jax.numpy as jnp
from jax import lax

TILE = 320
CW = 64
FB_DEV = 8
CT_DEV = 2
KT = 56
CAP = 5
NBLK = 2048
N_ROW = 16
N_COL = 16


def device_rows(key):
    first, second, third, fourth = jax.random.split(key, 4)
    total_slots = N_COL * CAP
    order = jax.random.permutation(first, total_slots).astype(jnp.int32)
    chosen_dest = jax.random.randint(second, (), 0, N_COL, dtype=jnp.int32)
    slot_dest = jnp.arange(total_slots, dtype=jnp.int32) // CAP
    score = order + jnp.where(slot_dest == chosen_dest, total_slots, 0).astype(jnp.int32)
    best_values, picked = lax.top_k(score, KT)
    mixing = jax.random.permutation(third, KT)
    picked = picked[mixing]
    dest = picked.astype(jnp.int32) // CAP
    within = jax.random.randint(fourth, (KT,), 0, FB_DEV, dtype=jnp.int32)
    return dest * FB_DEV + within


def draw_tile_rows(key, part):
    keys = jax.random.split(jax.random.fold_in(key, 17), N_ROW * N_COL)
    rows = jax.vmap(device_rows)(keys)
    return rows.reshape(N_ROW, N_COL, KT).astype(jnp.int32)


def set_ends(drawn, rng, low, largest):
    shape = drawn.shape
    place = [jax.random.randint(jax.random.fold_in(rng, axis), (), 0, shape[axis]) for axis in range(len(shape))]
    drawn = drawn.at[tuple(place)].set(low)
    longest = shape.index(max(shape))
    place[longest] = (place[longest] + 1) % shape[longest]
    return drawn.at[tuple(place)].set(largest)


def levels(own_key, shape, cuts, smallest, top_value):
    factor_of = 1.0
    for position, parts in cuts:
        steps = jax.random.uniform(jax.random.fold_in(jax.random.fold_in(own_key, 6), position), (parts,), jnp.float32, smallest / len(cuts), top_value / len(cuts))
        factor_of = factor_of * jnp.repeat(jnp.exp(steps), shape[position] // parts).reshape((-1,) + (1,) * (len(shape) - 1 - position))
    return factor_of


def scatter_about(stream_key, extent, width, bound, pieces=(), held_as=jnp.bfloat16):
    level = levels(stream_key, extent, pieces, -0.22, 0.18) if pieces else 1.0
    entries = jax.random.normal(stream_key, extent, jnp.float32) * width * level
    return jnp.minimum(jnp.maximum(entries, -bound), bound).astype(held_as)


def setup_inputs(seed: int = 0) -> dict:
    key_list = jax.random.split(jax.random.key(seed), 6)
    return {
        "jacobian": scatter_about(key_list[0], (N_ROW, N_COL, KT, TILE, TILE), 0.2, 3.0, ((0, 16), (1, 16))),
        "prolong": scatter_about(key_list[1], (NBLK, CW, TILE), TILE ** -0.5, 0.3125, ((0, 256),)),
        "tile_rows": draw_tile_rows(jax.random.fold_in(key_list[5], 71), 0),
        "tile_cols": set_ends(jax.random.randint(key_list[3], (N_ROW, N_COL, KT), 0, FB_DEV * N_ROW), jax.random.fold_in(key_list[3], 1), 0, (FB_DEV * N_ROW) - 1).astype(jnp.int32),
        "coarse_slot": set_ends(jax.random.randint(key_list[4], (N_ROW, N_COL, KT), 0, CT_DEV), jax.random.fold_in(key_list[4], 1), 0, CT_DEV - 1).astype(jnp.int32),
    }


def one_device(jacobian, prolong, rows, cols, slots, r, q):
    col_global = ((cols // FB_DEV) * N_COL + q) * FB_DEV + cols % FB_DEV
    row_global = (r * N_COL + rows // FB_DEV) * FB_DEV + rows % FB_DEV
    col_side = jnp.take(prolong, col_global.astype(jnp.int32), axis=0).astype(jnp.float32)
    row_side = jnp.take(prolong, row_global.astype(jnp.int32), axis=0).astype(jnp.float32)
    image = jnp.einsum("kab,kcb->kca", jacobian.astype(jnp.float32), col_side, precision=lax.Precision.HIGHEST).astype(jnp.bfloat16)
    part = jnp.einsum("kct,kdt->kcd", row_side, image.astype(jnp.float32), precision=lax.Precision.HIGHEST)
    target = ((rows // FB_DEV) * CT_DEV + slots).astype(jnp.int32)
    return jax.ops.segment_sum(part, target, num_segments=N_COL * CT_DEV)


def reference(jacobian, prolong, tile_rows, tile_cols, coarse_slot):
    def one_row(r):
        def one_col(q):
            return one_device(jacobian[r, q], prolong, tile_rows[r, q], tile_cols[r, q], coarse_slot[r, q], r, q)
        sums = lax.map(one_col, jnp.arange(N_COL, dtype=jnp.int32))
        total = jnp.sum(sums, axis=0)
        total = total.reshape(N_COL, CT_DEV, CW, CW).transpose(0, 2, 1, 3)
        return total.reshape(N_COL, CW, CT_DEV * CW)
    return lax.map(one_row, jnp.arange(N_ROW, dtype=jnp.int32))
```

```python
import functools

import jax
import jax.numpy as jnp
from jax import lax
from jax.experimental import pallas as pl
from jax.experimental.pallas import tpu as pltpu
from jax.sharding import PartitionSpec as P

MESH = pl.DeviceIdType.MESH
NX, NZL, NC, NZH, NY = 4, 2, 2, 4, 4
FB = 8
CAP = 5
PR, PC = 80, 256
HALF = FB // 2


def pack(p):
    t = p[:, 256:320]
    a = jnp.concatenate([t[0:16], t[16:32]], axis=1)
    b = jnp.concatenate([t[32:48], t[48:64]], axis=1)
    return jnp.concatenate([p[:, 0:256], jnp.concatenate([a, b], axis=1)], axis=0)


def unpack(v):
    q = v[64:80]
    tail = jnp.concatenate([q[:, 0:64], q[:, 64:128], q[:, 128:192], q[:, 192:256]], axis=0)
    return jnp.concatenate([v[0:64], tail], axis=1)


def kernel(
    jac, pro, rows, slots, cols, out,
    tiles, shard_in, colbuf, own, zm, zp, z2, picked, given, images, terms, landed,
    tab, tab_s, asked, asked_s, mask, local_sem, ask_sem, ss, rs,
):
    kt = tiles.shape[0]
    r = lax.axis_index("row")
    q = lax.axis_index("col")
    x, zl, c = r // 4, (r // 2) % 2, r % 2
    zh, y = q // NY, q % NY

    def dev(dx=0, dzl=0, dc=0, dzh=0, dy=0):
        return (
            ((x + dx) % NX) * 4 + ((zl + dzl) % NZL) * 2 + (c + dc) % NC,
            ((zh + dzh) % NZH) * NY + (y + dy) % NY,
        )

    def held(dx=0, dzl=0, dc=0):
        return (((x + dx) % NX) * 4 + ((zl + dzl) % NZL) * 2 + (c + dc) % NC) * FB

    sent = []
    count = [0]
    ids = {}

    def ident(name):
        if name not in ids:
            ids[name] = count[0]
            count[0] += 1
        return ids[name]

    def send(name, src, dst, to):
        i = ident(name)
        copy = pltpu.make_async_remote_copy(
            src_ref=src, dst_ref=dst, send_sem=ss.at[i], recv_sem=rs.at[i], device_id=to, device_id_type=MESH
        )
        copy.start()
        sent.append(copy)

    def arrive(name, dst):
        i = ident(name)
        pltpu.make_async_remote_copy(
            src_ref=dst, dst_ref=dst, send_sem=ss.at[i], recv_sem=rs.at[i], device_id=dev(dc=1), device_id_type=MESH
        ).wait_recv()

    get_tiles = pltpu.make_async_copy(jac, tiles, local_sem.at[0])
    get_shard = pltpu.make_async_copy(pro, shard_in, local_sem.at[1])
    get_shard.start()
    get_tiles.start()

    bar = pltpu.get_barrier_semaphore()
    peers = [dev(dc=1), dev(dzl=1), dev(dx=1), dev(dx=3)]
    peers += [dev(dzh=a, dy=b) for a in range(NZH) for b in range(NY) if (a, b) != (0, 0)]
    for peer in peers:
        pl.semaphore_signal(bar, inc=1, device_id=peer, device_id_type=MESH)

    row = rows[...]
    owner_row = jnp.right_shift(row, 3)
    block_row = jnp.bitwise_and(row, 7)
    sub = lax.broadcasted_iota(jnp.int32, (kt, kt), 0)
    lane = lax.broadcasted_iota(jnp.int32, (kt, kt), 1)
    diag = sub == lane
    owner_col = jnp.sum(jnp.where(diag, owner_row, 0), axis=1, keepdims=True)
    block_col = jnp.sum(jnp.where(diag, block_row, 0), axis=1, keepdims=True)
    same = owner_col == owner_row
    rank_col = jnp.sum(jnp.where(same & (lane < sub), 1, 0), axis=1, keepdims=True)
    rank_row = jnp.sum(jnp.where(same & (sub < lane), 1, 0), axis=0, keepdims=True)
    at_col = owner_col * 8 + rank_col
    at_row = owner_row * 8 + rank_row
    hot = at_col == lax.broadcasted_iota(jnp.int32, (kt, 128), 1)
    number = lax.broadcasted_iota(jnp.int32, (kt, 128), 0)
    tab[0:1, :] = jnp.sum(jnp.where(hot, number, 0), axis=0, keepdims=True)
    tab[1:2, :] = jnp.sum(jnp.where(hot, block_col, 0), axis=0, keepdims=True)
    tab[2:8, :] = jnp.zeros((6, 128), jnp.int32)
    put_tab = pltpu.make_async_copy(tab, tab_s, local_sem.at[2])
    put_tab.start()
    hot2 = at_row == lax.broadcasted_iota(jnp.int32, (128, kt), 0)
    which = jnp.sum(jnp.where(hot2, slots[...] + 1, 0), axis=1, keepdims=True)
    half = jnp.right_shift(lax.broadcasted_iota(jnp.int32, (128, 128), 1), 6) + 1
    mask[...] = jnp.where(half == which, 1.0, 0.0)

    get_shard.wait()
    mine = held()
    for b in range(FB):
        v = pack(shard_in[b])
        own[b] = v
        colbuf[mine + b] = v

    pl.semaphore_wait(bar, len(peers))

    def slot_of(at, first=0, n=FB):
        return colbuf.at[pl.ds(at + first, n)]

    for dy in range(1, NY):
        send(f"ask{dy}", tab, asked.at[dy - 1], dev(dy=dy))
    send("zl", own, slot_of(mine), dev(dzl=1))
    send("xp", own, slot_of(mine), dev(dx=1))
    send("xm", own, slot_of(mine), dev(dx=3))
    send("zp", own, zm, dev(dzh=1))
    send("zm", own, zp, dev(dzh=3))
    send("sib", own, slot_of(mine), dev(dc=1))

    put_tab.wait()
    asks = []
    for dy in range(1, NY):
        arrive(f"ask{dy}", asked.at[dy - 1])
        copy = pltpu.make_async_copy(asked.at[dy - 1], asked_s.at[dy - 1], ask_sem.at[dy - 1])
        copy.start()
        asks.append(copy)
    for copy in asks:
        copy.wait()

    def hand_out(dz, shard):
        owner = ((zh + dz) % NZH) * NY + y
        for d in (1, 3, 2):
            to = NY - d
            for j in range(CAP):
                picked[dz, to - 1, j] = shard[asked_s[d - 1, 1, owner * 8 + j]]
            send(f"y{dz}{to}", picked.at[dz, to - 1], given.at[dz, to - 1], dev(dy=to))

    hand_out(0, own)

    def across(tag, dzl):
        at = held(dx=3, dzl=dzl)
        arrive(f"xp{tag}", slot_of(at))
        send(f"xpp{tag}", slot_of(at, 0, HALF), slot_of(at, 0, HALF), dev(dx=1))
        send(f"sxp{tag}", slot_of(at), slot_of(at), dev(dc=1))
        at = held(dx=1, dzl=dzl)
        arrive(f"xm{tag}", slot_of(at))
        send(f"xmm{tag}", slot_of(at, HALF, HALF), slot_of(at, HALF, HALF), dev(dx=3))
        send(f"sxm{tag}", slot_of(at), slot_of(at), dev(dc=1))

    def beyond(tag, dzl):
        at = held(dx=2, dzl=dzl)
        arrive(f"xpp{tag}", slot_of(at, 0, HALF))
        arrive(f"xmm{tag}", slot_of(at, HALF, HALF))
        send(f"sx2{tag}", slot_of(at), slot_of(at), dev(dc=1))

    across("", 0)
    at = held(dzl=1)
    arrive("zl", slot_of(at))
    send("xp1", slot_of(at), slot_of(at), dev(dx=1))
    send("xm1", slot_of(at), slot_of(at), dev(dx=3))
    send("szl", slot_of(at), slot_of(at), dev(dc=1))
    beyond("", 0)

    arrive("zp", zm)
    send("zpp", zm.at[pl.ds(0, HALF)], z2.at[pl.ds(0, HALF)], dev(dzh=1))
    arrive("zm", zp)
    send("zmm", zp.at[pl.ds(HALF, HALF)], z2.at[pl.ds(HALF, HALF)], dev(dzh=3))
    hand_out(3, zm)
    hand_out(1, zp)

    across("1", 1)
    arrive("zpp", z2.at[pl.ds(0, HALF)])
    arrive("zmm", z2.at[pl.ds(HALF, HALF)])
    hand_out(2, z2)
    beyond("1", 1)

    at = held(dc=1)
    arrive("sib", slot_of(at))
    for tag, dzl in (("", 0), ("1", 1)):
        for name, dx in (("sxp", 3), ("sxm", 1), ("sx2", 2)):
            at = held(dx=dx, dzl=dzl, dc=1)
            arrive(name + tag, slot_of(at))
    at = held(dzl=1, dc=1)
    arrive("szl", slot_of(at))
    get_tiles.wait()

    def image(k, carry):
        p = unpack(colbuf[cols[0, k]])
        pp = jnp.concatenate([p, p], axis=0)
        images[k] = lax.dot_general(
            tiles[k], pp, (((1,), (1,)), ((), ())), preferred_element_type=jnp.float32
        ).astype(jnp.bfloat16)
        return carry

    lax.fori_loop(0, kt, image, 0, unroll=2)

    shards = {0: own, 1: zp, 2: z2, 3: zm}
    here = None
    for dz in (0, 3, 1, 2):
        for dy in (0, 1, 3, 2):
            o = ((zh + dz) % NZH) * NY + (y + dy) % NY
            if dy:
                arrive(f"y{dz}{NY - dy}", given.at[dz, NY - dy - 1])
            m = mask[pl.ds(pl.multiple_of(o * 8, 8), 8), :]
            total = None
            for j in range(CAP):
                if dy:
                    v = given[dz, NY - dy - 1, j]
                else:
                    v = shards[dz][tab_s[1, o * 8 + j]]
                part = jnp.dot(unpack(v), images[tab_s[0, o * 8 + j]], preferred_element_type=jnp.float32)
                part = part * m[j : j + 1, :]
                total = part if total is None else total + part
            i = dz * NY + dy
            terms[i] = total
            if i:
                send(f"t{i}", terms.at[i], landed.at[i], dev(dzh=dz, dy=dy))

    total = terms[0]
    for dz in (0, 3, 1, 2):
        for dy in (0, 1, 3, 2):
            i = dz * NY + dy
            if i:
                arrive(f"t{i}", landed.at[i])
                total = total + landed[i]
    out[...] = total
    for copy in sent:
        copy.wait_send()


MESSAGES = 3 + 1 + 4 + 4 + 8 + 4 + 12 + 15


def per_device(jacobian, prolong, tile_rows, tile_cols, coarse_slot):
    kt, tile = jacobian.shape[2], jacobian.shape[3]
    vmem = pl.BlockSpec(memory_space=pltpu.VMEM)
    bf = jnp.bfloat16
    result = pl.pallas_call(
        kernel,
        out_shape=jax.ShapeDtypeStruct((64, 128), jnp.float32),
        in_specs=[
            pl.BlockSpec(memory_space=pl.ANY),
            pl.BlockSpec(memory_space=pl.ANY),
            vmem,
            vmem,
            pl.BlockSpec(memory_space=pltpu.SMEM),
        ],
        out_specs=vmem,
        scratch_shapes=[
            pltpu.VMEM((kt, tile, tile), bf),
            pltpu.VMEM((FB, 64, tile), bf),
            pltpu.VMEM((16 * FB, PR, PC), bf),
            pltpu.VMEM((FB, PR, PC), bf),
            pltpu.VMEM((FB, PR, PC), bf),
            pltpu.VMEM((FB, PR, PC), bf),
            pltpu.VMEM((FB, PR, PC), bf),
            pltpu.VMEM((NZH, NY - 1, CAP, PR, PC), bf),
            pltpu.VMEM((NZH, NY - 1, CAP, PR, PC), bf),
            pltpu.VMEM((kt, tile, 128), bf),
            pltpu.VMEM((16, 64, 128), jnp.float32),
            pltpu.VMEM((16, 64, 128), jnp.float32),
            pltpu.VMEM((8, 128), jnp.int32),
            pltpu.SMEM((8, 128), jnp.int32),
            pltpu.VMEM((NY - 1, 8, 128), jnp.int32),
            pltpu.SMEM((NY - 1, 8, 128), jnp.int32),
            pltpu.VMEM((128, 128), jnp.float32),
            pltpu.SemaphoreType.DMA((3,)),
            pltpu.SemaphoreType.DMA((NY - 1,)),
            pltpu.SemaphoreType.DMA((MESSAGES,)),
            pltpu.SemaphoreType.DMA((MESSAGES,)),
        ],
        compiler_params=pltpu.CompilerParams(
            collective_id=0, has_side_effects=True, vmem_limit_bytes=56 * 2**20
        ),
        name="coarse_operator",
    )(
        jacobian.reshape(kt, tile, tile),
        prolong,
        tile_rows.reshape(1, kt),
        coarse_slot.reshape(1, kt),
        tile_cols.reshape(1, kt),
    )
    return result.reshape(1, 1, 64, 128)


def solution(mesh):
    placed = (
        P("row", "col", None, None, None),
        P(("row", "col"), None, None),
        P("row", "col", None),
        P("row", "col", None),
        P("row", "col", None),
    )
    return jax.shard_map(
        per_device,
        mesh=mesh,
        in_specs=placed,
        out_specs=P("row", "col", None, None),
        check_vma=False,
    )
```

```python
import functools

import jax
import jax.numpy as jnp
from jax import lax
from jax.experimental import pallas as pl
from jax.experimental.pallas import tpu as pltpu
from jax.sharding import PartitionSpec as P

MESH = pl.DeviceIdType.MESH
NX, NZL, NC, NZH, NY = 4, 2, 2, 4, 4
FB = 8
CAP = 5
PR, PC = 80, 256
HALF = FB // 2
CUT = ((0, 48), (48, 32))


def pack(p):
    t = p[:, 256:320]
    a = jnp.concatenate([t[0:16], t[16:32]], axis=1)
    b = jnp.concatenate([t[32:48], t[48:64]], axis=1)
    return jnp.concatenate([p[:, 0:256], jnp.concatenate([a, b], axis=1)], axis=0)


def unpack(v):
    q = v[64:80]
    tail = jnp.concatenate([q[:, 0:64], q[:, 64:128], q[:, 128:192], q[:, 192:256]], axis=0)
    return jnp.concatenate([v[0:64], tail], axis=1)


def kernel(
    jac, pro, rows, slots, cols, out,
    tiles, shard_in, colbuf, own, zm0, zm1, zp0, zp1, z2, picked, given, images, terms, landed,
    tab, tab_s, asked, asked_s, mask, local_sem, ask_sem, ss, rs,
):
    kt = tiles.shape[0]
    r = lax.axis_index("row")
    q = lax.axis_index("col")
    x, zl, c = r // 4, (r // 2) % 2, r % 2
    zh, y = q // NY, q % NY

    def dev(dx=0, dzl=0, dc=0, dzh=0, dy=0):
        return (
            ((x + dx) % NX) * 4 + ((zl + dzl) % NZL) * 2 + (c + dc) % NC,
            ((zh + dzh) % NZH) * NY + (y + dy) % NY,
        )

    def held(dx=0, dzl=0, dc=0):
        return (((x + dx) % NX) * 4 + ((zl + dzl) % NZL) * 2 + (c + dc) % NC) * FB

    sent = []
    count = [0]
    ids = {}

    def ident(name):
        if name not in ids:
            ids[name] = count[0]
            count[0] += 1
        return ids[name]

    def send(name, src, dst, to):
        i = ident(name)
        copy = pltpu.make_async_remote_copy(
            src_ref=src, dst_ref=dst, send_sem=ss.at[i], recv_sem=rs.at[i], device_id=to, device_id_type=MESH
        )
        copy.start()
        sent.append(copy)

    def arrive(name, dst):
        i = ident(name)
        pltpu.make_async_remote_copy(
            src_ref=dst, dst_ref=dst, send_sem=ss.at[i], recv_sem=rs.at[i], device_id=dev(dc=1), device_id_type=MESH
        ).wait_recv()

    get_tiles = pltpu.make_async_copy(jac, tiles, local_sem.at[0])
    get_shard = pltpu.make_async_copy(pro, shard_in, local_sem.at[1])
    get_shard.start()
    get_tiles.start()

    bar = pltpu.get_barrier_semaphore()
    peers = [dev(dc=1), dev(dzl=1), dev(dx=1), dev(dx=3)]
    peers += [dev(dzh=a, dy=b) for a in range(NZH) for b in range(NY) if (a, b) in ((0,1),(0,2),(0,3),(1,0),(3,0))]
    for peer in peers:
        pl.semaphore_signal(bar, inc=1, device_id=peer, device_id_type=MESH)

    row = rows[...]
    owner_row = jnp.right_shift(row, 3)
    block_row = jnp.bitwise_and(row, 7)
    sub = lax.broadcasted_iota(jnp.int32, (kt, kt), 0)
    lane = lax.broadcasted_iota(jnp.int32, (kt, kt), 1)
    diag = sub == lane
    owner_col = jnp.sum(jnp.where(diag, owner_row, 0), axis=1, keepdims=True)
    block_col = jnp.sum(jnp.where(diag, block_row, 0), axis=1, keepdims=True)
    same = owner_col == owner_row
    rank_col = jnp.sum(jnp.where(same & (lane < sub), 1, 0), axis=1, keepdims=True)
    rank_row = jnp.sum(jnp.where(same & (sub < lane), 1, 0), axis=0, keepdims=True)
    at_col = owner_col * 8 + rank_col
    at_row = owner_row * 8 + rank_row
    hot = at_col == lax.broadcasted_iota(jnp.int32, (kt, 128), 1)
    number = lax.broadcasted_iota(jnp.int32, (kt, 128), 0)
    tab[0:1, :] = jnp.sum(jnp.where(hot, number, 0), axis=0, keepdims=True)
    tab[1:2, :] = jnp.sum(jnp.where(hot, block_col, 0), axis=0, keepdims=True)
    tab[2:8, :] = jnp.zeros((6, 128), jnp.int32)
    put_tab = pltpu.make_async_copy(tab, tab_s, local_sem.at[2])
    put_tab.start()
    hot2 = at_row == lax.broadcasted_iota(jnp.int32, (128, kt), 0)
    which = jnp.sum(jnp.where(hot2, slots[...] + 1, 0), axis=1, keepdims=True)
    half = jnp.right_shift(lax.broadcasted_iota(jnp.int32, (128, 128), 1), 6) + 1
    mask[...] = jnp.where(half == which, 1.0, 0.0)

    get_shard.wait()
    mine = held()
    for b in range(FB):
        v = pack(shard_in[b])
        own[b] = v
        colbuf[mine + b] = v

    pl.semaphore_wait(bar, len(peers))

    def slot_of(at, first=0, n=FB):
        return colbuf.at[pl.ds(at + first, n)]

    for dy in range(1, NY):
        send(f"ask{dy}", tab, asked.at[dy - 1], dev(dy=dy))
    zms, zps = (zm0, zm1), (zp0, zp1)

    def lend(ch):
        first, n = CUT[ch]
        part = own.at[:, pl.ds(first, n)]
        send(f"zp{ch}", part, zms[ch], dev(dzh=1))
        send(f"zm{ch}", part, zps[ch], dev(dzh=3))

    lend(0)
    send("xp", own, slot_of(mine), dev(dx=1))
    send("xm", own, slot_of(mine), dev(dx=3))
    send("sib", own, slot_of(mine), dev(dc=1))

    put_tab.wait()
    asks = []
    for dy in range(1, NY):
        arrive(f"ask{dy}", asked.at[dy - 1])
        copy = pltpu.make_async_copy(asked.at[dy - 1], asked_s.at[dy - 1], ask_sem.at[dy - 1])
        copy.start()
        asks.append(copy)
    for copy in asks:
        copy.wait()

    def hand_out(dz, shard, first=0, n=PR):
        owner = ((zh + dz) % NZH) * NY + y
        rows_of = pl.ds(first, n)
        for d in (1, 3, 2):
            to = NY - d
            for j in range(CAP):
                picked[dz, to - 1, j, rows_of] = shard[asked_s[d - 1, 1, owner * 8 + j]]
            send(
                f"y{dz}{to}{first}",
                picked.at[dz, to - 1, :, rows_of],
                given.at[dz, to - 1, :, rows_of],
                dev(dy=to),
            )

    hand_out(0, own)

    def borrow(ch):
        arrive(f"zp{ch}", zms[ch])
        arrive(f"zm{ch}", zps[ch])

    def pass_on(ch):
        at = pl.ds(*CUT[ch])
        send(f"zpp{ch}", zms[ch].at[pl.ds(0, HALF)], z2.at[pl.ds(0, HALF), at], dev(dzh=1))
        send(f"zmm{ch}", zps[ch].at[pl.ds(HALF, HALF)], z2.at[pl.ds(HALF, HALF), at], dev(dzh=3))

    def hand_on(ch):
        hand_out(3, zms[ch], *CUT[ch])
        hand_out(1, zps[ch], *CUT[ch])

    def get_far():
        for ch in (0, 1):
            at = pl.ds(*CUT[ch])
            arrive(f"zpp{ch}", z2.at[pl.ds(0, HALF), at])
            arrive(f"zmm{ch}", z2.at[pl.ds(HALF, HALF), at])

    def get_zl():
        at = held(dzl=1)
        arrive("zl", slot_of(at))
        send("xp1", slot_of(at), slot_of(at), dev(dx=1))
        send("xm1", slot_of(at), slot_of(at), dev(dx=3))
        send("szl", slot_of(at), slot_of(at), dev(dc=1))

    def put_zl():
        send("zl", own, slot_of(mine), dev(dzl=1))

    def across(tag, dzl):
        at = held(dx=3, dzl=dzl)
        arrive(f"xp{tag}", slot_of(at))
        send(f"xpp{tag}", slot_of(at, 0, HALF), slot_of(at, 0, HALF), dev(dx=1))
        send(f"sxp{tag}", slot_of(at), slot_of(at), dev(dc=1))
        at = held(dx=1, dzl=dzl)
        arrive(f"xm{tag}", slot_of(at))
        send(f"xmm{tag}", slot_of(at, HALF, HALF), slot_of(at, HALF, HALF), dev(dx=3))
        send(f"sxm{tag}", slot_of(at), slot_of(at), dev(dc=1))

    def beyond(tag, dzl):
        at = held(dx=2, dzl=dzl)
        arrive(f"xpp{tag}", slot_of(at, 0, HALF))
        arrive(f"xmm{tag}", slot_of(at, HALF, HALF))
        send(f"sx2{tag}", slot_of(at), slot_of(at), dev(dc=1))

    put_zl()
    borrow(0)
    hand_on(0)
    across("", 0)
    get_zl()
    lend(1)
    pass_on(0)
    beyond("", 0)
    borrow(1)
    pass_on(1)
    hand_on(1)
    across("1", 1)
    get_far()
    hand_out(2, z2)
    beyond("1", 1)
    at = held(dc=1)
    arrive("sib", slot_of(at))
    for tag, dzl in (("", 0), ("1", 1)):
        for name, dx in (("sxp", 3), ("sxm", 1), ("sx2", 2)):
            at = held(dx=dx, dzl=dzl, dc=1)
            arrive(name + tag, slot_of(at))
    at = held(dzl=1, dc=1)
    arrive("szl", slot_of(at))
    get_tiles.wait()

    def image(k, carry):
        p = unpack(colbuf[cols[0, k]])
        pp = jnp.concatenate([p, p], axis=0)
        images[k] = lax.dot_general(
            tiles[k], pp, (((1,), (1,)), ((), ())), preferred_element_type=jnp.float32
        ).astype(jnp.bfloat16)
        return carry

    lax.fori_loop(0, kt, image, 0, unroll=14)

    def kept(dz, b):
        if dz in (1, 3):
            return jnp.concatenate([part[b] for part in (zps if dz == 1 else zms)], axis=0)
        return (z2 if dz else own)[b]

    here = None
    for dz in (0, 3, 1, 2):
        for dy in (0, 1, 3, 2):
            o = ((zh + dz) % NZH) * NY + (y + dy) % NY
            if dy:
                for first, n in CUT if dz in (1, 3) else ((0, PR),):
                    arrive(f"y{dz}{NY - dy}{first}", given.at[dz, NY - dy - 1, :, pl.ds(first, n)])
            m = mask[pl.ds(pl.multiple_of(o * 8, 8), 8), :]
            total = None
            for j in range(CAP):
                if dy:
                    v = given[dz, NY - dy - 1, j]
                else:
                    v = kept(dz, tab_s[1, o * 8 + j])
                part = jnp.dot(unpack(v), images[tab_s[0, o * 8 + j]], preferred_element_type=jnp.float32)
                part = part * m[j : j + 1, :]
                total = part if total is None else total + part
            i = dz * NY + dy
            terms[i] = total.astype(jnp.bfloat16)
            if not i: here = total
            if i:
                send(f"t{i}", terms.at[i], landed.at[i], dev(dzh=dz, dy=dy))

    total = here
    for dz in (0, 3, 1, 2):
        for dy in (0, 1, 3, 2):
            i = dz * NY + dy
            if i:
                arrive(f"t{i}", landed.at[i])
                total = total + landed[i].astype(jnp.float32)
    out[...] = total
    for copy in sent:
        copy.wait_send()


MESSAGES = 3 + 1 + 4 + 8 + 8 + 4 + 18 + 15


def per_device(jacobian, prolong, tile_rows, tile_cols, coarse_slot):
    kt, tile = jacobian.shape[2], jacobian.shape[3]
    vmem = pl.BlockSpec(memory_space=pltpu.VMEM)
    bf = jnp.bfloat16
    result = pl.pallas_call(
        kernel,
        out_shape=jax.ShapeDtypeStruct((64, 128), jnp.float32),
        in_specs=[
            pl.BlockSpec(memory_space=pl.ANY),
            pl.BlockSpec(memory_space=pl.ANY),
            vmem,
            vmem,
            pl.BlockSpec(memory_space=pltpu.SMEM),
        ],
        out_specs=vmem,
        scratch_shapes=[
            pltpu.VMEM((kt, tile, tile), bf),
            pltpu.VMEM((FB, 64, tile), bf),
            pltpu.VMEM((16 * FB, PR, PC), bf),
            pltpu.VMEM((FB, PR, PC), bf),
            pltpu.VMEM((FB, CUT[0][1], PC), bf),
            pltpu.VMEM((FB, CUT[1][1], PC), bf),
            pltpu.VMEM((FB, CUT[0][1], PC), bf),
            pltpu.VMEM((FB, CUT[1][1], PC), bf),
            pltpu.VMEM((FB, PR, PC), bf),
            pltpu.VMEM((NZH, NY - 1, CAP, PR, PC), bf),
            pltpu.VMEM((NZH, NY - 1, CAP, PR, PC), bf),
            pltpu.VMEM((kt, tile, 128), bf),
            pltpu.VMEM((16, 64, 128), bf),
            pltpu.VMEM((16, 64, 128), bf),
            pltpu.VMEM((8, 128), jnp.int32),
            pltpu.SMEM((8, 128), jnp.int32),
            pltpu.VMEM((NY - 1, 8, 128), jnp.int32),
            pltpu.SMEM((NY - 1, 8, 128), jnp.int32),
            pltpu.VMEM((128, 128), jnp.float32),
            pltpu.SemaphoreType.DMA((3,)),
            pltpu.SemaphoreType.DMA((NY - 1,)),
            pltpu.SemaphoreType.DMA((MESSAGES,)),
            pltpu.SemaphoreType.DMA((MESSAGES,)),
        ],
        compiler_params=pltpu.CompilerParams(
            collective_id=0, has_side_effects=True, vmem_limit_bytes=56 * 2**20
        ),
        name="coarse_operator",
    )(
        jacobian.reshape(kt, tile, tile),
        prolong,
        tile_rows.reshape(1, kt),
        coarse_slot.reshape(1, kt),
        tile_cols.reshape(1, kt),
    )
    return result.reshape(1, 1, 64, 128)


def solution(mesh):
    placed = (
        P("row", "col", None, None, None),
        P(("row", "col"), None, None),
        P("row", "col", None),
        P("row", "col", None),
        P("row", "col", None),
    )
    return jax.shard_map(
        per_device,
        mesh=mesh,
        in_specs=placed,
        out_specs=P("row", "col", None, None),
        check_vma=False,
    )
```

```python
import functools

import jax
import jax.numpy as jnp
from jax import lax
from jax.experimental import pallas as pl
from jax.experimental.pallas import tpu as pltpu
from jax.sharding import PartitionSpec as P

MESH = pl.DeviceIdType.MESH
NX, NZL, NC, NZH, NY = 4, 2, 2, 4, 4
FB = 8
CAP = 5
PR, PC = 80, 256
HALF = FB // 2
CUT = ((0, 64), (64, 16))


def pack(p):
    t = p[:, 256:320]
    a = jnp.concatenate([t[0:16], t[16:32]], axis=1)
    b = jnp.concatenate([t[32:48], t[48:64]], axis=1)
    return jnp.concatenate([p[:, 0:256], jnp.concatenate([a, b], axis=1)], axis=0)


def unpack(v):
    q = v[64:80]
    tail = jnp.concatenate([q[:, 0:64], q[:, 64:128], q[:, 128:192], q[:, 192:256]], axis=0)
    return jnp.concatenate([v[0:64], tail], axis=1)


def kernel(
    jac, pro, rows, slots, cols, out,
    tiles, shard_in, colbuf, own, zm0, zm1, zp0, zp1, z2, picked, given, images, terms, landed,
    tab, tab_s, asked, asked_s, mask, local_sem, ask_sem, ss, rs,
):
    kt = tiles.shape[0]
    r = lax.axis_index("row")
    q = lax.axis_index("col")
    x, zl, c = r // 4, (r // 2) % 2, r % 2
    zh, y = q // NY, q % NY

    xs = [(x + d) % NX for d in range(NX)]
    zls = [zl, 1 - zl]
    cs = [c, 1 - c]
    zhs = [(zh + d) % NZH for d in range(NZH)]
    ys = [(y + d) % NY for d in range(NY)]

    def dev(dx=0, dzl=0, dc=0, dzh=0, dy=0):
        return xs[dx] * 4 + zls[dzl] * 2 + cs[dc], zhs[dzh] * NY + ys[dy]

    def held(dx=0, dzl=0, dc=0):
        return (xs[dx] * 4 + zls[dzl] * 2 + cs[dc]) * FB

    sent = []
    count = [0]
    ids = {}

    def ident(name):
        if name not in ids:
            ids[name] = count[0]
            count[0] += 1
        return ids[name]

    def send(name, src, dst, to):
        i = ident(name)
        copy = pltpu.make_async_remote_copy(
            src_ref=src, dst_ref=dst, send_sem=ss.at[i], recv_sem=rs.at[i], device_id=to, device_id_type=MESH
        )
        copy.start()
        sent.append(copy)

    def arrive(name, dst):
        i = ident(name)
        pltpu.make_async_remote_copy(
            src_ref=dst, dst_ref=dst, send_sem=ss.at[i], recv_sem=rs.at[i], device_id=dev(dc=1), device_id_type=MESH
        ).wait_recv()

    get_tiles = pltpu.make_async_copy(jac, tiles, local_sem.at[0])
    get_shard = pltpu.make_async_copy(pro, shard_in, local_sem.at[1])
    get_shard.start()
    get_tiles.start()

    bar = pltpu.get_barrier_semaphore()
    peers = [dev(dc=1), dev(dzl=1), dev(dx=1), dev(dx=3)]
    peers += [dev(dzh=a, dy=b) for a in range(NZH) for b in range(NY) if (a, b) in ((0,1),(0,2),(0,3),(1,0),(3,0))]
    for peer in peers:
        pl.semaphore_signal(bar, inc=1, device_id=peer, device_id_type=MESH)

    row = rows[...]
    owner_row = jnp.right_shift(row, 3)
    block_row = jnp.bitwise_and(row, 7)
    sub = lax.broadcasted_iota(jnp.int32, (kt, kt), 0)
    lane = lax.broadcasted_iota(jnp.int32, (kt, kt), 1)
    diag = sub == lane
    owner_col = jnp.sum(jnp.where(diag, owner_row, 0), axis=1, keepdims=True)
    block_col = jnp.sum(jnp.where(diag, block_row, 0), axis=1, keepdims=True)
    same = owner_col == owner_row
    rank_col = jnp.sum(jnp.where(same & (lane < sub), 1, 0), axis=1, keepdims=True)
    rank_row = jnp.sum(jnp.where(same & (sub < lane), 1, 0), axis=0, keepdims=True)
    at_col = owner_col * 8 + rank_col
    at_row = owner_row * 8 + rank_row
    hot = at_col == lax.broadcasted_iota(jnp.int32, (kt, 128), 1)
    number = lax.broadcasted_iota(jnp.int32, (kt, 128), 0)
    tab[0:1, :] = jnp.sum(jnp.where(hot, number, 0), axis=0, keepdims=True)
    tab[1:2, :] = jnp.sum(jnp.where(hot, block_col, 0), axis=0, keepdims=True)
    tab[2:8, :] = jnp.zeros((6, 128), jnp.int32)
    put_tab = pltpu.make_async_copy(tab, tab_s, local_sem.at[2])
    put_tab.start()
    hot2 = at_row == lax.broadcasted_iota(jnp.int32, (128, kt), 0)
    which = jnp.sum(jnp.where(hot2, slots[...] + 1, 0), axis=1, keepdims=True)
    half = jnp.right_shift(lax.broadcasted_iota(jnp.int32, (128, 128), 1), 6) + 1
    mask[...] = jnp.where(half == which, 1.0, 0.0)

    get_shard.wait()
    mine = held()
    for b in range(FB):
        v = pack(shard_in[b])
        own[b] = v
        colbuf[mine + b] = v

    pl.semaphore_wait(bar, len(peers))

    def slot_of(at, first=0, n=FB):
        return colbuf.at[pl.ds(at + first, n)]

    for dy in range(1, NY):
        send(f"ask{dy}", tab, asked.at[dy - 1], dev(dy=dy))
    zms, zps = (zm0, zm1), (zp0, zp1)

    def lend(ch):
        first, n = CUT[ch]
        part = own.at[:, pl.ds(first, n)]
        send(f"zp{ch}", part, zms[ch], dev(dzh=1))
        send(f"zm{ch}", part, zps[ch], dev(dzh=3))

    lend(0)
    send("xp", own, slot_of(mine), dev(dx=1))
    send("xm", own, slot_of(mine), dev(dx=3))
    send("sib", own, slot_of(mine), dev(dc=1))

    put_tab.wait()
    asks = []
    for dy in range(1, NY):
        arrive(f"ask{dy}", asked.at[dy - 1])
        copy = pltpu.make_async_copy(asked.at[dy - 1], asked_s.at[dy - 1], ask_sem.at[dy - 1])
        copy.start()
        asks.append(copy)
    for copy in asks:
        copy.wait()

    def hand_out(dz, shard, first=0, n=PR):
        owner = zhs[dz] * NY + y
        rows_of = pl.ds(first, n)
        for d in (1, 3, 2):
            to = NY - d
            for j in range(CAP):
                picked[dz, to - 1, j, rows_of] = shard[asked_s[d - 1, 1, owner * 8 + j]]
            send(
                f"y{dz}{to}{first}",
                picked.at[dz, to - 1, :, rows_of],
                given.at[dz, to - 1, :, rows_of],
                dev(dy=to),
            )

    hand_out(0, own)

    def borrow(ch):
        arrive(f"zp{ch}", zms[ch])
        arrive(f"zm{ch}", zps[ch])

    def pass_on(ch):
        at = pl.ds(*CUT[ch])
        send(f"zpp{ch}", zms[ch].at[pl.ds(0, HALF)], z2.at[pl.ds(0, HALF), at], dev(dzh=1))
        send(f"zmm{ch}", zps[ch].at[pl.ds(HALF, HALF)], z2.at[pl.ds(HALF, HALF), at], dev(dzh=3))

    def hand_on(ch):
        hand_out(3, zms[ch], *CUT[ch])
        hand_out(1, zps[ch], *CUT[ch])

    def get_far():
        for ch in (0, 1):
            at = pl.ds(*CUT[ch])
            arrive(f"zpp{ch}", z2.at[pl.ds(0, HALF), at])
            arrive(f"zmm{ch}", z2.at[pl.ds(HALF, HALF), at])

    def get_zl():
        at = held(dzl=1)
        arrive("zl", slot_of(at))
        send("xp1", slot_of(at), slot_of(at), dev(dx=1))
        send("xm1", slot_of(at), slot_of(at), dev(dx=3))
        send("szl", slot_of(at), slot_of(at), dev(dc=1))

    def put_zl():
        send("zl", own, slot_of(mine), dev(dzl=1))

    def across(tag, dzl):
        at = held(dx=3, dzl=dzl)
        arrive(f"xp{tag}", slot_of(at))
        send(f"xpp{tag}", slot_of(at, 0, HALF), slot_of(at, 0, HALF), dev(dx=1))
        send(f"sxp{tag}", slot_of(at), slot_of(at), dev(dc=1))
        at = held(dx=1, dzl=dzl)
        arrive(f"xm{tag}", slot_of(at))
        send(f"xmm{tag}", slot_of(at, HALF, HALF), slot_of(at, HALF, HALF), dev(dx=3))
        send(f"sxm{tag}", slot_of(at), slot_of(at), dev(dc=1))

    def beyond(tag, dzl):
        at = held(dx=2, dzl=dzl)
        arrive(f"xpp{tag}", slot_of(at, 0, HALF))
        arrive(f"xmm{tag}", slot_of(at, HALF, HALF))
        send(f"sx2{tag}", slot_of(at), slot_of(at), dev(dc=1))

    put_zl()
    borrow(0)
    hand_on(0)
    across("", 0)
    get_zl()
    lend(1)
    pass_on(0)
    beyond("", 0)
    borrow(1)
    pass_on(1)
    hand_on(1)
    across("1", 1)
    get_far()
    hand_out(2, z2)
    beyond("1", 1)
    at = held(dc=1)
    arrive("sib", slot_of(at))
    for tag, dzl in (("", 0), ("1", 1)):
        for name, dx in (("sxp", 3), ("sxm", 1), ("sx2", 2)):
            at = held(dx=dx, dzl=dzl, dc=1)
            arrive(name + tag, slot_of(at))
    at = held(dzl=1, dc=1)
    arrive("szl", slot_of(at))
    get_tiles.wait()

    def image(k, carry):
        p = unpack(colbuf[cols[0, k]])
        pp = jnp.concatenate([p, p], axis=0)
        images[k] = lax.dot_general(
            tiles[k], pp, (((1,), (1,)), ((), ())), preferred_element_type=jnp.float32
        ).astype(jnp.bfloat16)
        return carry

    lax.fori_loop(0, kt, image, 0, unroll=28)

    def kept(dz, b):
        if dz in (1, 3):
            return jnp.concatenate([part[b] for part in (zps if dz == 1 else zms)], axis=0)
        return (z2 if dz else own)[b]

    here = None
    turns = [(dz, 0) for dz in (2, 3, 1, 0)] + [(dz, dy) for dz in (0, 3, 1, 2) for dy in (2, 1, 3)]
    for dz, dy in turns:
            o = zhs[dz] * NY + ys[dy]
            if dy:
                for first, n in CUT if dz in (1, 3) else ((0, PR),):
                    arrive(f"y{dz}{NY - dy}{first}", given.at[dz, NY - dy - 1, :, pl.ds(first, n)])
            m = mask[pl.ds(pl.multiple_of(o * 8, 8), 8), :]
            total = None
            for j in range(CAP):
                if dy:
                    v = given[dz, NY - dy - 1, j]
                else:
                    v = kept(dz, tab_s[1, o * 8 + j])
                part = jnp.dot(unpack(v), images[tab_s[0, o * 8 + j]], preferred_element_type=jnp.float32)
                part = part * m[j : j + 1, :]
                total = part if total is None else total + part
            i = dz * NY + dy
            terms[i] = total.astype(jnp.bfloat16)
            if not i: here = total
            if i:
                send(f"t{i}", terms.at[i], landed.at[i], dev(dzh=dz, dy=dy))

    total = here
    for dz in (0, 3, 1, 2):
        for dy in (0, 1, 3, 2):
            i = dz * NY + dy
            if i:
                arrive(f"t{i}", landed.at[i])
                total = total + landed[i].astype(jnp.float32)
    out[...] = total
    for copy in sent:
        copy.wait_send()


MESSAGES = 3 + 1 + 4 + 8 + 8 + 4 + 18 + 15


def per_device(jacobian, prolong, tile_rows, tile_cols, coarse_slot):
    kt, tile = jacobian.shape[2], jacobian.shape[3]
    vmem = pl.BlockSpec(memory_space=pltpu.VMEM)
    bf = jnp.bfloat16
    result = pl.pallas_call(
        kernel,
        out_shape=jax.ShapeDtypeStruct((64, 128), jnp.float32),
        in_specs=[
            pl.BlockSpec(memory_space=pl.ANY),
            pl.BlockSpec(memory_space=pl.ANY),
            vmem,
            vmem,
            pl.BlockSpec(memory_space=pltpu.SMEM),
        ],
        out_specs=vmem,
        scratch_shapes=[
            pltpu.VMEM((kt, tile, tile), bf),
            pltpu.VMEM((FB, 64, tile), bf),
            pltpu.VMEM((16 * FB, PR, PC), bf),
            pltpu.VMEM((FB, PR, PC), bf),
            pltpu.VMEM((FB, CUT[0][1], PC), bf),
            pltpu.VMEM((FB, CUT[1][1], PC), bf),
            pltpu.VMEM((FB, CUT[0][1], PC), bf),
            pltpu.VMEM((FB, CUT[1][1], PC), bf),
            pltpu.VMEM((FB, PR, PC), bf),
            pltpu.VMEM((NZH, NY - 1, CAP, PR, PC), bf),
            pltpu.VMEM((NZH, NY - 1, CAP, PR, PC), bf),
            pltpu.VMEM((kt, tile, 128), bf),
            pltpu.VMEM((16, 64, 128), bf),
            pltpu.VMEM((16, 64, 128), bf),
            pltpu.VMEM((8, 128), jnp.int32),
            pltpu.SMEM((8, 128), jnp.int32),
            pltpu.VMEM((NY - 1, 8, 128), jnp.int32),
            pltpu.SMEM((NY - 1, 8, 128), jnp.int32),
            pltpu.VMEM((128, 128), jnp.float32),
            pltpu.SemaphoreType.DMA((3,)),
            pltpu.SemaphoreType.DMA((NY - 1,)),
            pltpu.SemaphoreType.DMA((MESSAGES,)),
            pltpu.SemaphoreType.DMA((MESSAGES,)),
        ],
        compiler_params=pltpu.CompilerParams(
            collective_id=0, has_side_effects=True, vmem_limit_bytes=56 * 2**20
        ),
        name="coarse_operator",
    )(
        jacobian.reshape(kt, tile, tile),
        prolong,
        tile_rows.reshape(1, kt),
        coarse_slot.reshape(1, kt),
        tile_cols.reshape(1, kt),
    )
    return result.reshape(1, 1, 64, 128)


def solution(mesh):
    placed = (
        P("row", "col", None, None, None),
        P(("row", "col"), None, None),
        P("row", "col", None),
        P("row", "col", None),
        P("row", "col", None),
    )
    return jax.shard_map(
        per_device,
        mesh=mesh,
        in_specs=placed,
        out_specs=P("row", "col", None, None),
        check_vma=False,
    )
```

```python
import functools

import jax
import jax.numpy as jnp
from jax import lax
from jax.experimental import pallas as pl
from jax.experimental.pallas import tpu as pltpu
from jax.sharding import PartitionSpec as P

MESH = pl.DeviceIdType.MESH
NX, NZL, NC, NZH, NY = 4, 2, 2, 4, 4
FB = 8
CAP = 5
PR, PC = 80, 256
HALF = FB // 2
CUT = ((0, 48), (48, 32))
EARLY = 32


def pack(p):
    t = p[:, 256:320]
    a = jnp.concatenate([t[0:16], t[16:32]], axis=1)
    b = jnp.concatenate([t[32:48], t[48:64]], axis=1)
    return jnp.concatenate([p[:, 0:256], jnp.concatenate([a, b], axis=1)], axis=0)


def unpack(v):
    q = v[64:80]
    tail = jnp.concatenate([q[:, 0:64], q[:, 64:128], q[:, 128:192], q[:, 192:256]], axis=0)
    return jnp.concatenate([v[0:64], tail], axis=1)


def kernel(
    jac, pro, rows, slots, cols, out,
    tiles, shard_in, colbuf, own, zm0, zm1, zp0, zp1, z20, z21, ahead, picked, given, images, terms, landed,
    tab, tab_s, asked, asked_s, mask, local_sem, ask_sem, ss, rs,
):
    kt = tiles.shape[0]
    r = lax.axis_index("row")
    q = lax.axis_index("col")
    x, zl, c = r // 4, (r // 2) % 2, r % 2
    zh, y = q // NY, q % NY

    xs = [(x + d) % NX for d in range(NX)]
    zls = [zl, 1 - zl]
    cs = [c, 1 - c]
    zhs = [(zh + d) % NZH for d in range(NZH)]
    ys = [(y + d) % NY for d in range(NY)]

    def dev(dx=0, dzl=0, dc=0, dzh=0, dy=0):
        return xs[dx] * 4 + zls[dzl] * 2 + cs[dc], zhs[dzh] * NY + ys[dy]

    def held(dx=0, dzl=0, dc=0):
        return (xs[dx] * 4 + zls[dzl] * 2 + cs[dc]) * FB

    sent = []
    count = [0]
    ids = {}

    def ident(name):
        if name not in ids:
            ids[name] = count[0]
            count[0] += 1
        return ids[name]

    def send(name, src, dst, to):
        i = ident(name)
        copy = pltpu.make_async_remote_copy(
            src_ref=src, dst_ref=dst, send_sem=ss.at[i], recv_sem=rs.at[i], device_id=to, device_id_type=MESH
        )
        copy.start()
        sent.append(copy)

    def arrive(name, dst):
        i = ident(name)
        pltpu.make_async_remote_copy(
            src_ref=dst, dst_ref=dst, send_sem=ss.at[i], recv_sem=rs.at[i], device_id=dev(dc=1), device_id_type=MESH
        ).wait_recv()

    get_tiles = pltpu.make_async_copy(jac, tiles, local_sem.at[0])
    get_shard = pltpu.make_async_copy(pro, shard_in, local_sem.at[1])
    get_shard.start()
    get_tiles.start()

    bar = pltpu.get_barrier_semaphore()
    peers = [dev(dc=1), dev(dzl=1), dev(dx=1), dev(dx=3)]
    peers += [dev(dzh=a, dy=b) for a in range(NZH) for b in range(NY) if (a, b) in ((0,1),(0,2),(0,3),(1,0),(3,0))]
    for peer in peers:
        pl.semaphore_signal(bar, inc=1, device_id=peer, device_id_type=MESH)

    row = rows[...]
    owner_row = jnp.right_shift(row, 3)
    block_row = jnp.bitwise_and(row, 7)
    sub = lax.broadcasted_iota(jnp.int32, (kt, kt), 0)
    lane = lax.broadcasted_iota(jnp.int32, (kt, kt), 1)
    diag = sub == lane
    owner_col = jnp.sum(jnp.where(diag, owner_row, 0), axis=1, keepdims=True)
    block_col = jnp.sum(jnp.where(diag, block_row, 0), axis=1, keepdims=True)
    same = owner_col == owner_row
    rank_col = jnp.sum(jnp.where(same & (lane < sub), 1, 0), axis=1, keepdims=True)
    rank_row = jnp.sum(jnp.where(same & (sub < lane), 1, 0), axis=0, keepdims=True)
    at_col = owner_col * 8 + rank_col
    at_row = owner_row * 8 + rank_row
    hot = at_col == lax.broadcasted_iota(jnp.int32, (kt, 128), 1)
    number = lax.broadcasted_iota(jnp.int32, (kt, 128), 0)
    tab[0:1, :] = jnp.sum(jnp.where(hot, number, 0), axis=0, keepdims=True)
    tab[1:2, :] = jnp.sum(jnp.where(hot, block_col, 0), axis=0, keepdims=True)
    tab[2:8, :] = jnp.zeros((6, 128), jnp.int32)
    put_tab = pltpu.make_async_copy(tab, tab_s, local_sem.at[2])
    put_tab.start()
    hot2 = at_row == lax.broadcasted_iota(jnp.int32, (128, kt), 0)
    which = jnp.sum(jnp.where(hot2, slots[...] + 1, 0), axis=1, keepdims=True)
    half = jnp.right_shift(lax.broadcasted_iota(jnp.int32, (128, 128), 1), 6) + 1
    mask[...] = jnp.where(half == which, 1.0, 0.0)

    get_shard.wait()
    mine = held()
    for b in range(FB):
        v = pack(shard_in[b])
        own[b] = v
        colbuf[mine + b] = v

    pl.semaphore_wait(bar, len(peers))

    def slot_of(at, first=0, n=FB):
        return colbuf.at[pl.ds(at + first, n)]

    for dy in range(1, NY):
        send(f"ask{dy}", tab, asked.at[dy - 1], dev(dy=dy))
    zms, zps, z2s = (zm0, zm1), (zp0, zp1), (z20, z21)

    def lend(ch):
        first, n = CUT[ch]
        part = own.at[:, pl.ds(first, n)]
        send(f"zp{ch}", part, zms[ch], dev(dzh=1))
        send(f"zm{ch}", part, zps[ch], dev(dzh=3))

    for dy in (2, 1, 3):
        send(f"e{dy}", own.at[:, pl.ds(0, EARLY)], ahead.at[dy - 1], dev(dy=dy))
    lend(0)
    send("xp", own, slot_of(mine), dev(dx=1))
    send("xm", own, slot_of(mine), dev(dx=3))
    send("sib", own, slot_of(mine), dev(dc=1))

    put_tab.wait()
    asks = []
    for dy in range(1, NY):
        arrive(f"ask{dy}", asked.at[dy - 1])
        copy = pltpu.make_async_copy(asked.at[dy - 1], asked_s.at[dy - 1], ask_sem.at[dy - 1])
        copy.start()
        asks.append(copy)
    for copy in asks:
        copy.wait()

    def hand_out(dz, shard, first=0, n=PR):
        owner = zhs[dz] * NY + y
        rows_of = pl.ds(first, n)
        for d in (1, 3, 2):
            to = NY - d
            for j in range(CAP):
                picked[dz, to - 1, j, rows_of] = shard[asked_s[d - 1, 1, owner * 8 + j]]
            send(
                f"y{dz}{to}{first}",
                picked.at[dz, to - 1, :, rows_of],
                given.at[dz, to - 1, :, rows_of],
                dev(dy=to),
            )

    hand_out(0, own.at[:, pl.ds(EARLY, PR - EARLY)], EARLY, PR - EARLY)

    def borrow(ch):
        arrive(f"zp{ch}", zms[ch])
        arrive(f"zm{ch}", zps[ch])

    def pass_on(ch):
        far = z2s[ch]
        send(f"zpp{ch}", zms[ch].at[pl.ds(0, HALF)], far.at[pl.ds(0, HALF)], dev(dzh=1))
        send(f"zmm{ch}", zps[ch].at[pl.ds(HALF, HALF)], far.at[pl.ds(HALF, HALF)], dev(dzh=3))

    def hand_on(ch):
        hand_out(3, zms[ch], *CUT[ch])
        hand_out(1, zps[ch], *CUT[ch])

    def get_far(ch):
        arrive(f"zpp{ch}", z2s[ch].at[pl.ds(0, HALF)])
        arrive(f"zmm{ch}", z2s[ch].at[pl.ds(HALF, HALF)])
        hand_out(2, z2s[ch], *CUT[ch])

    def get_zl():
        at = held(dzl=1)
        arrive("zl", slot_of(at))
        send("xp1", slot_of(at), slot_of(at), dev(dx=1))
        send("xm1", slot_of(at), slot_of(at), dev(dx=3))
        send("szl", slot_of(at), slot_of(at), dev(dc=1))

    def put_zl():
        send("zl", own, slot_of(mine), dev(dzl=1))

    def across(tag, dzl):
        at = held(dx=3, dzl=dzl)
        arrive(f"xp{tag}", slot_of(at))
        send(f"xpp{tag}", slot_of(at, 0, HALF), slot_of(at, 0, HALF), dev(dx=1))
        send(f"sxp{tag}", slot_of(at), slot_of(at), dev(dc=1))
        at = held(dx=1, dzl=dzl)
        arrive(f"xm{tag}", slot_of(at))
        send(f"xmm{tag}", slot_of(at, HALF, HALF), slot_of(at, HALF, HALF), dev(dx=3))
        send(f"sxm{tag}", slot_of(at), slot_of(at), dev(dc=1))

    def beyond(tag, dzl):
        at = held(dx=2, dzl=dzl)
        arrive(f"xpp{tag}", slot_of(at, 0, HALF))
        arrive(f"xmm{tag}", slot_of(at, HALF, HALF))
        send(f"sx2{tag}", slot_of(at), slot_of(at), dev(dc=1))

    put_zl()
    borrow(0)
    hand_on(0)
    across("", 0)
    get_zl()
    lend(1)
    pass_on(0)
    beyond("", 0)
    borrow(1)
    pass_on(1)
    hand_on(1)
    across("1", 1)
    get_far(0)
    get_far(1)
    beyond("1", 1)
    at = held(dc=1)
    arrive("sib", slot_of(at))
    for tag, dzl in (("", 0), ("1", 1)):
        for name, dx in (("sxp", 3), ("sxm", 1), ("sx2", 2)):
            at = held(dx=dx, dzl=dzl, dc=1)
            arrive(name + tag, slot_of(at))
    at = held(dzl=1, dc=1)
    arrive("szl", slot_of(at))
    get_tiles.wait()

    def image(k, carry):
        p = unpack(colbuf[cols[0, k]])
        pp = jnp.concatenate([p, p], axis=0)
        images[k] = lax.dot_general(
            tiles[k], pp, (((1,), (1,)), ((), ())), preferred_element_type=jnp.float32
        ).astype(jnp.bfloat16)
        return carry

    lax.fori_loop(0, kt, image, 0, unroll=28)

    def kept(dz, b):
        if dz:
            return jnp.concatenate([part[b] for part in (None, zps, z2s, zms)[dz]], axis=0)
        return own[b]

    here = None
    for dy in range(1, NY):
        arrive(f"e{dy}", ahead.at[dy - 1])
    turns = [(dz, 0) for dz in (2, 3, 1, 0)] + [(dz, dy) for dz in (0, 3, 1, 2) for dy in (2, 1, 3)]
    for dz, dy in turns:
            o = zhs[dz] * NY + ys[dy]
            if dy:
                for first, n in {0: ((EARLY, PR - EARLY),)}.get(dz, CUT):
                    arrive(f"y{dz}{NY - dy}{first}", given.at[dz, NY - dy - 1, :, pl.ds(first, n)])
            m = mask[pl.ds(pl.multiple_of(o * 8, 8), 8), :]
            total = None
            for j in range(CAP):
                if dy:
                    v = given[dz, NY - dy - 1, j]
                    if not dz:
                        first = ahead[NY - dy - 1, tab_s[1, o * 8 + j]]
                        v = jnp.concatenate([first, v[EARLY:]], axis=0)
                else:
                    v = kept(dz, tab_s[1, o * 8 + j])
                part = jnp.dot(unpack(v), images[tab_s[0, o * 8 + j]], preferred_element_type=jnp.float32)
                part = part * m[j : j + 1, :]
                total = part if total is None else total + part
            i = dz * NY + dy
            terms[i] = total.astype(jnp.bfloat16)
            if not i: here = total
            if i:
                send(f"t{i}", terms.at[i], landed.at[i], dev(dzh=dz, dy=dy))

    total = here
    for dz in (0, 3, 1, 2):
        for dy in (0, 1, 3, 2):
            i = dz * NY + dy
            if i:
                arrive(f"t{i}", landed.at[i])
                total = total + landed[i].astype(jnp.float32)
    out[...] = total
    for copy in sent:
        copy.wait_send()


MESSAGES = 3 + 3 + 1 + 4 + 8 + 8 + 4 + 21 + 15


def per_device(jacobian, prolong, tile_rows, tile_cols, coarse_slot):
    kt, tile = jacobian.shape[2], jacobian.shape[3]
    vmem = pl.BlockSpec(memory_space=pltpu.VMEM)
    bf = jnp.bfloat16
    result = pl.pallas_call(
        kernel,
        out_shape=jax.ShapeDtypeStruct((64, 128), jnp.float32),
        in_specs=[
            pl.BlockSpec(memory_space=pl.ANY),
            pl.BlockSpec(memory_space=pl.ANY),
            vmem,
            vmem,
            pl.BlockSpec(memory_space=pltpu.SMEM),
        ],
        out_specs=vmem,
        scratch_shapes=[
            pltpu.VMEM((kt, tile, tile), bf),
            pltpu.VMEM((FB, 64, tile), bf),
            pltpu.VMEM((16 * FB, PR, PC), bf),
            pltpu.VMEM((FB, PR, PC), bf),
            pltpu.VMEM((FB, CUT[0][1], PC), bf),
            pltpu.VMEM((FB, CUT[1][1], PC), bf),
            pltpu.VMEM((FB, CUT[0][1], PC), bf),
            pltpu.VMEM((FB, CUT[1][1], PC), bf),
            pltpu.VMEM((FB, CUT[0][1], PC), bf),
            pltpu.VMEM((FB, CUT[1][1], PC), bf),
            pltpu.VMEM((NY - 1, FB, EARLY, PC), bf),
            pltpu.VMEM((NZH, NY - 1, CAP, PR, PC), bf),
            pltpu.VMEM((NZH, NY - 1, CAP, PR, PC), bf),
            pltpu.VMEM((kt, tile, 128), bf),
            pltpu.VMEM((16, 64, 128), bf),
            pltpu.VMEM((16, 64, 128), bf),
            pltpu.VMEM((8, 128), jnp.int32),
            pltpu.SMEM((8, 128), jnp.int32),
            pltpu.VMEM((NY - 1, 8, 128), jnp.int32),
            pltpu.SMEM((NY - 1, 8, 128), jnp.int32),
            pltpu.VMEM((128, 128), jnp.float32),
            pltpu.SemaphoreType.DMA((3,)),
            pltpu.SemaphoreType.DMA((NY - 1,)),
            pltpu.SemaphoreType.DMA((MESSAGES,)),
            pltpu.SemaphoreType.DMA((MESSAGES,)),
        ],
        compiler_params=pltpu.CompilerParams(
            collective_id=0, has_side_effects=True, vmem_limit_bytes=56 * 2**20
        ),
        name="coarse_operator",
    )(
        jacobian.reshape(kt, tile, tile),
        prolong,
        tile_rows.reshape(1, kt),
        coarse_slot.reshape(1, kt),
        tile_cols.reshape(1, kt),
    )
    return result.reshape(1, 1, 64, 128)


def solution(mesh):
    placed = (
        P("row", "col", None, None, None),
        P(("row", "col"), None, None),
        P("row", "col", None),
        P("row", "col", None),
        P("row", "col", None),
    )
    return jax.shard_map(
        per_device,
        mesh=mesh,
        in_specs=placed,
        out_specs=P("row", "col", None, None),
        check_vma=False,
    )
```
